32 devices in a mesh: dp: 4 (over y, x), expert: 8 (over z, core).
Axes of the slice: x: 2, y: 2, z: 4, core: 2. Of those that a mesh axis runs over, the one named last changes fastest.
Arguments:
- tokens: bfloat16 [4096, 2048], P(('dp', 'expert')), may hold values from -6 to 6
- cotangent: bfloat16 [4096, 2048], P(('dp', 'expert')), may hold values from -6 to 6
- expert_ids: int32 [4096, 4], P(('dp', 'expert')), may hold values from 0 to 7, all different within a row; in each aligned block of 128 rows (0 to 127, 128 to 255, ...) at most 96 rows name the same one
- gate_probs: bfloat16 [4096, 4], P(('dp', 'expert')), may hold values from 0.049804688 to 0.5
- w_in: bfloat16 [8, 2048, 1536], P('expert', 'dp'), may hold values from -0.125 to 0.125
- w_out: bfloat16 [8, 768, 2048], P('expert', 'dp'), may hold values from -0.21875 to 0.21875
- mom_in: float32 [8, 2048, 1536], P('expert', 'dp'), may hold values from -12 to 12
- mom_out: float32 [8, 768, 2048], P('expert', 'dp'), may hold values from -12 to 12
Outputs:
- layer_out: bfloat16 [4096, 2048], P(('dp', 'expert'))
- tokens_grad: bfloat16 [4096, 2048], P(('dp', 'expert'))
- gate_grad: bfloat16 [4096, 4], P(('dp', 'expert'))
- w_in_new: bfloat16 [8, 2048, 1536], P('expert', 'dp')
- w_out_new: bfloat16 [8, 768, 2048], P('expert', 'dp')
- mom_in_new: float32 [8, 2048, 1536], P('expert', 'dp')
- mom_out_new: float32 [8, 768, 2048], P('expert', 'dp')
The draws below stay inside these ranges and needn't reach their ends.
Inputs may be any that keep to these rules, and one draw needn't show every extreme that they name: `expert_ids`: each row names 4 different experts. Among the 128 tokens of one device (aligned blocks of rows), no expert is named more than 96 times, a bound that some block reaches.
All inputs are finite; a program needn't handle non-finite values.
Results may differ from the reference program's by a relative error of at most 0.009.
Values may be sent and summed in bfloat16 or wider, within the bound.
A program may use at most 128 MiB of HBM per device.

```python
import math
import jax
import jax.numpy as jnp
import numpy as np
from jax import lax

D = 2048
FF = 768
TOP = 4
TOK_DEV = 128
EXPERTS = 8
CAP = 96
SLOTS = 768
TOKENS = 4096
N_DP = 4
N_EXPERT = 8


def shard_levels(key, shape, pieces, smallest, largest):
    def one(axis_at, parts):
        steps = jax.random.uniform(jax.random.fold_in(jax.random.fold_in(key, 6), axis_at), (parts,), jnp.float32, smallest / len(pieces), largest / len(pieces))
        return jnp.repeat(jnp.exp(steps), shape[axis_at] // parts).reshape((-1,) + (1,) * (len(shape) - axis_at - 1))

    loudness = one(*pieces[0])
    for cut in pieces[1:]:
        loudness = loudness * one(*cut)
    return loudness


def routed_block(rng, own, number, rows, amount, top, reach, skew):
    order = jax.random.permutation(rng, amount)
    heavy_load, usual = load_shares(amount, rows * top, reach, skew, True), load_shares(amount, rows * top, reach, skew, False)
    places = jnp.arange(amount)

    def named(lengths, offset_by):
        used = int((lengths > 0).sum())
        fixed = max(1, used // 4)
        passed = fixed + (places - fixed + offset_by * (used - fixed)) % max(1, amount - fixed)
        return jnp.zeros((amount,), jnp.int32).at[order[jnp.where(places < fixed, places, passed)]].set(jnp.asarray(lengths, jnp.int32))

    lengths = jnp.where(number % 4 == 0, named(heavy_load, number // 4), named(usual, number - number // 4 - 1))
    mixed = jax.random.permutation(jax.random.fold_in(own, 3), amount)
    donor, taker = mixed[0:amount // 2 * 2:2], mixed[1:amount // 2 * 2:2]
    slack = jnp.minimum(lengths[donor] - 1, reach - lengths[taker]) // 2
    slack = jnp.where((donor == order[0]) | (taker == order[0]) | (lengths[taker] == 0), 0, jnp.maximum(slack, 0))
    passed = jax.random.randint(jax.random.fold_in(own, 4), (amount // 2,), 0, 1 << 20) % (slack + 1)
    lengths = lengths.at[donor].add(-passed).at[taker].add(passed)
    members = jnp.searchsorted(jnp.cumsum(lengths), jnp.arange(rows * top), side="right").astype(jnp.int32)
    grid = members.reshape(top, rows).T
    grid = grid[jax.random.permutation(jax.random.fold_in(own, 1), rows)]
    offset_by = jax.random.randint(jax.random.fold_in(own, 2), (rows, 1), 0, top)
    return jnp.take_along_axis(grid, (jnp.arange(top)[None, :] + offset_by) % top, axis=1)


def load_shares(amount, total, bound, lean, full):
    weights = [(1 << 20) // math.isqrt(grade ** lean) + 1 for grade in range(1, amount + 1)]
    largest = bound if full else min(bound, max(-(-total // amount), total * weights[0] // sum(weights)))
    least = 1 if total - largest >= amount - 1 else 0
    holding, spare = [largest] + [least] * (amount - 1), total - largest - least * (amount - 1)
    while spare > 0:
        candidates = [i for i in range(1, amount) if holding[i] < largest] or [i for i in range(1, amount) if holding[i] < bound]
        pool, budget = sum([weights[i] for i in candidates]), spare
        for i in candidates:
            addition = min(bound - holding[i], max(1, budget * weights[i] // pool), spare)
            holding[i] = holding[i] + addition
            spare = spare - addition
    return np.array(holding)


def bell_draw(own_key, extent, deviation, most, cuts=(), kind=jnp.bfloat16):
    drawn = deviation * jax.random.normal(own_key, extent, jnp.float32)
    if cuts:
        drawn = drawn * shard_levels(own_key, extent, cuts, -0.22, 0.18)
    return jnp.clip(drawn, -most, most).astype(kind)


def setup_inputs(seed: int = 0) -> dict:
    key_list = jax.random.split(jax.random.key(seed), 9)
    tokens = bell_draw(key_list[0], (TOKENS, D), 1.0, 6.0, ((0, 32),))
    cotangent = bell_draw(key_list[1], (TOKENS, D), 1.0, 6.0, ((0, 32),))
    expert_ids_keys = jax.random.split(jax.random.fold_in(key_list[2], 1), TOKENS // TOK_DEV)
    expert_ids_turns = jax.random.permutation(jax.random.fold_in(key_list[2], 3), TOKENS // TOK_DEV)
    expert_ids = jax.vmap(lambda own, number: routed_block(jax.random.fold_in(key_list[2], 2), own, number, TOK_DEV, EXPERTS, TOP, CAP, 2))(expert_ids_keys, expert_ids_turns).reshape((TOKENS, TOP))
    gate_probs = jnp.clip(0.049804688 + 0.4501953 * jax.random.uniform(key_list[3], (TOKENS, TOP), jnp.float32) ** shard_levels(key_list[3], (TOKENS, TOP), ((0, 32),), -0.2, 0.2), 0.049804688, 0.5).astype(jnp.bfloat16)
    w_in = bell_draw(key_list[4], (EXPERTS, D, 2 * FF), D ** -0.5, 0.125, ((0, 8), (1, 4)))
    w_out = bell_draw(key_list[5], (EXPERTS, FF, D), FF ** -0.5, 0.21875, ((0, 8), (1, 4)))
    mom_in = bell_draw(key_list[6], (EXPERTS, D, 2 * FF), 2.0, 12.0, ((0, 8), (1, 4)), jnp.float32)
    mom_out = bell_draw(key_list[7], (EXPERTS, FF, D), 2.0, 12.0, ((0, 8), (1, 4)), jnp.float32)
    return {"tokens": tokens, "cotangent": cotangent, "expert_ids": expert_ids, "gate_probs": gate_probs, "w_in": w_in, "w_out": w_out, "mom_in": mom_in, "mom_out": mom_out}


beta_one = 0.9
beta_two = 0.99
learn_rate = 0.02
decay_rate = 0.1

def expert_pass(inputs, cots, gates, weight_in, weight_out):
    pre = jnp.einsum('erd,edf->erf', inputs.astype(jnp.float32), weight_in.astype(jnp.float32))
    gate_part = pre[..., :FF]
    up_part = pre[..., FF:]
    sig_part = jax.nn.sigmoid(gate_part)
    activated = gate_part * sig_part
    hidden = (activated * up_part).astype(jnp.bfloat16)
    expert_out = jnp.einsum('erf,efd->erd', hidden.astype(jnp.float32), weight_out.astype(jnp.float32))
    gate_col = gates.astype(jnp.float32)[..., None]
    weighted = (gate_col * expert_out).astype(jnp.bfloat16)
    slot_gate = lax.optimization_barrier(jnp.sum(cots.astype(jnp.float32) * expert_out, axis=-1)).astype(jnp.bfloat16)
    out_grad = (gate_col * cots.astype(jnp.float32)).astype(jnp.bfloat16)
    hidden_grad = jnp.einsum('erd,efd->erf', out_grad.astype(jnp.float32), weight_out.astype(jnp.float32))
    slope = sig_part * (1.0 + gate_part * (1.0 - sig_part))
    pre_grad = jnp.concatenate([hidden_grad * up_part * slope, hidden_grad * activated], axis=-1).astype(jnp.bfloat16)
    slot_grad = jnp.einsum('erf,edf->erd', pre_grad.astype(jnp.float32), weight_in.astype(jnp.float32)).astype(jnp.bfloat16)
    part_in = jnp.einsum('erd,erf->edf', inputs.astype(jnp.float32), pre_grad.astype(jnp.float32)).astype(jnp.bfloat16)
    part_out = jnp.einsum('erf,erd->efd', hidden.astype(jnp.float32), out_grad.astype(jnp.float32)).astype(jnp.bfloat16)
    return (weighted, slot_gate, slot_grad, part_in, part_out)

def lion_update(weight, moment, grad):
    blend = beta_one * moment + (1.0 - beta_one) * grad
    direction = blend / jnp.sqrt(blend * blend + 1.0)
    wide = weight.astype(jnp.float32)
    new_weight = (wide - learn_rate * (direction + decay_rate * wide)).astype(jnp.bfloat16)
    new_moment = beta_two * moment + (1.0 - beta_two) * grad
    return (new_weight, new_moment)

def reference(tokens, cotangent, expert_ids, gate_probs, w_in, w_out, mom_in, mom_out):
    blocks = N_DP * N_EXPERT
    pairs = TOK_DEV * TOP
    replica_rows = N_EXPERT * TOK_DEV
    expert_rows = expert_ids.reshape(blocks, pairs)
    onehot = (expert_rows[:, :, None] == jnp.arange(EXPERTS, dtype=jnp.int32)[None, None, :]).astype(jnp.int32)
    position = lax.optimization_barrier(jnp.sum((jnp.cumsum(onehot, axis=1) - onehot) * onehot, axis=2))
    source = (jnp.arange(blocks, dtype=jnp.int32) % N_EXPERT)[:, None]
    slot_index = (expert_rows * SLOTS + source * CAP + position).astype(jnp.int32).reshape(N_DP, N_EXPERT * pairs)
    replica_tokens = tokens.reshape(N_DP, replica_rows, D)
    replica_cots = cotangent.reshape(N_DP, replica_rows, D)
    replica_gates = gate_probs.reshape(N_DP, N_EXPERT * pairs)
    owner_row = jnp.repeat(jnp.arange(replica_rows, dtype=jnp.int32), TOP)
    total = EXPERTS * SLOTS

    def replica(carry, item):
        slots, rows_in, rows_cot, gates = item
        inputs = jnp.zeros((total, D), rows_in.dtype).at[slots].set(rows_in[owner_row]).reshape(EXPERTS, SLOTS, D)
        cots = jnp.zeros((total, D), rows_cot.dtype).at[slots].set(rows_cot[owner_row]).reshape(EXPERTS, SLOTS, D)
        gate_buf = jnp.zeros((total,), gates.dtype).at[slots].set(gates).reshape(EXPERTS, SLOTS)
        weighted, slot_gate, slot_grad, part_in, part_out = expert_pass(inputs, cots, gate_buf, w_in, w_out)
        layer_rows = lax.optimization_barrier(jnp.sum(weighted.reshape(total, D)[slots].astype(jnp.float32).reshape(replica_rows, TOP, D), axis=1)).astype(jnp.bfloat16)
        grad_rows = lax.optimization_barrier(jnp.sum(slot_grad.reshape(total, D)[slots].astype(jnp.float32).reshape(replica_rows, TOP, D), axis=1)).astype(jnp.bfloat16)
        gate_rows = slot_gate.reshape(total)[slots].reshape(replica_rows, TOP)
        new_carry = (carry[0] + part_in.astype(jnp.float32), carry[1] + part_out.astype(jnp.float32))
        return (new_carry, (layer_rows, grad_rows, gate_rows))
    start = (jnp.zeros((EXPERTS, D, 2 * FF), jnp.float32), jnp.zeros((EXPERTS, FF, D), jnp.float32))
    sums, outputs = lax.scan(replica, start, (slot_index, replica_tokens, replica_cots, replica_gates))
    grad_in, grad_out = sums
    layer_out = outputs[0].reshape(TOKENS, D)
    tokens_grad = outputs[1].reshape(TOKENS, D)
    gate_grad = outputs[2].reshape(TOKENS, TOP)
    w_in_new, mom_in_new = lion_update(w_in, mom_in, grad_in)
    w_out_new, mom_out_new = lion_update(w_out, mom_out, grad_out)
    return (layer_out, tokens_grad, gate_grad, w_in_new, w_out_new, mom_in_new, mom_out_new)
```

```python
import jax
import jax.numpy as jnp
from jax import lax
from jax.sharding import PartitionSpec as P

FF = 768


beta_one = 0.9
beta_two = 0.99
learn_rate = 0.02
decay_rate = 0.1


def lion_update(weight, moment, grad):
    blend = beta_one * moment + (1.0 - beta_one) * grad
    direction = blend / jnp.sqrt(blend * blend + 1.0)
    wide = weight.astype(jnp.float32)
    new_weight = (wide - learn_rate * (direction + decay_rate * wide)).astype(jnp.bfloat16)
    new_moment = beta_two * moment + (1.0 - beta_two) * grad
    return (new_weight, new_moment)


def dot(a, b, contract):
    return lax.dot_general(a, b, (contract, ((), ())), preferred_element_type=jnp.float32)


def body(tokens, cotangent, expert_ids, gate_probs, w_in, w_out, mom_in, mom_out):
    groups = lax.axis_size("expert")
    me = lax.axis_index("expert")
    tok_rows = tokens.shape[0]
    rows = lax.all_gather(tokens, "expert", axis=0, tiled=True)
    cots = lax.all_gather(cotangent, "expert", axis=0, tiled=True)
    hits = (expert_ids[:, :, None] == jnp.arange(groups, dtype=jnp.int32)[None, None, :])
    gates = jnp.sum(jnp.where(hits, gate_probs.astype(jnp.float32)[:, :, None], 0.0), axis=1)
    gates = lax.all_to_all(
        gates.astype(jnp.bfloat16).T.reshape(groups, tok_rows), "expert", 0, 0, tiled=True
    )
    gate_col = gates.reshape(-1).astype(jnp.float32)[:, None]
    full_in = lax.all_gather(w_in[0], "dp", axis=0, tiled=True)
    full_out = lax.all_gather(w_out[0], "dp", axis=0, tiled=True)

    pre = dot(rows, full_in, ((1,), (0,)))
    gate_part = pre[:, :FF]
    up_part = pre[:, FF:]
    sig_part = jax.nn.sigmoid(gate_part)
    activated = gate_part * sig_part
    hidden = (activated * up_part).astype(jnp.bfloat16)
    out_grad = (gate_col * cots.astype(jnp.float32)).astype(jnp.bfloat16)
    term_out = dot(hidden, out_grad, ((0,), (0,))).astype(jnp.bfloat16)
    grad_out = lax.psum_scatter(term_out, "dp", scatter_dimension=0, tiled=True)
    expert_out = dot(hidden, full_out, ((1,), (0,)))
    weighted = (gate_col * expert_out).astype(jnp.bfloat16)
    slot_gate = jnp.sum(cots.astype(jnp.float32) * expert_out, axis=-1).astype(jnp.bfloat16)
    layer_out = lax.psum_scatter(weighted, "expert", scatter_dimension=0, tiled=True)
    gate_back = lax.all_to_all(slot_gate.reshape(groups, tok_rows), "expert", 0, 0, tiled=True)
    hidden_grad = dot(out_grad, full_out, ((1,), (1,)))
    slope = sig_part * (1.0 + gate_part * (1.0 - sig_part))
    pre_grad = jnp.concatenate(
        [hidden_grad * up_part * slope, hidden_grad * activated], axis=-1
    ).astype(jnp.bfloat16)
    term_in = dot(rows, pre_grad, ((0,), (0,))).astype(jnp.bfloat16)
    grad_in = lax.psum_scatter(term_in, "dp", scatter_dimension=0, tiled=True)
    slot_grad = dot(pre_grad, full_in, ((1,), (1,))).astype(jnp.bfloat16)
    tokens_grad = lax.psum_scatter(slot_grad, "expert", scatter_dimension=0, tiled=True)
    gate_grad = jnp.sum(
        jnp.where(hits, gate_back.astype(jnp.float32).T[:, None, :], 0.0), axis=2
    ).astype(jnp.bfloat16)
    w_in_new, mom_in_new = lion_update(w_in, mom_in, grad_in.astype(jnp.float32)[None])
    w_out_new, mom_out_new = lion_update(w_out, mom_out, grad_out.astype(jnp.float32)[None])
    return (layer_out, tokens_grad, gate_grad, w_in_new, w_out_new, mom_in_new, mom_out_new)


def solution(mesh):
    rows_spec = P(("dp", "expert"), None)
    weight_spec = P("expert", "dp", None)
    in_specs = (rows_spec,) * 4 + (weight_spec,) * 4
    out_specs = (rows_spec,) * 3 + (weight_spec,) * 4
    return jax.shard_map(body, mesh=mesh, in_specs=in_specs, out_specs=out_specs, check_vma=False)
```

```python
import functools

import jax
import jax.numpy as jnp
from jax import lax
from jax.experimental import pallas as pl
from jax.experimental.pallas import tpu as pltpu
from jax.sharding import PartitionSpec as P

FF = 768


beta_one = 0.9
beta_two = 0.99
learn_rate = 0.02
decay_rate = 0.1


def lion_update(weight, moment, grad):
    blend = beta_one * moment + (1.0 - beta_one) * grad
    direction = blend / jnp.sqrt(blend * blend + 1.0)
    wide = weight.astype(jnp.float32)
    new_weight = (wide - learn_rate * (direction + decay_rate * wide)).astype(jnp.bfloat16)
    new_moment = beta_two * moment + (1.0 - beta_two) * grad
    return (new_weight, new_moment)


def dot(a, b, contract):
    return lax.dot_general(a, b, (contract, ((), ())), preferred_element_type=jnp.float32)


def body(tokens, cotangent, expert_ids, gate_probs, w_in, w_out, mom_in, mom_out):
    groups = lax.axis_size("expert")
    me = lax.axis_index("expert")
    tok_rows = tokens.shape[0]
    rows = lax.all_gather(tokens, "expert", axis=0, tiled=True)
    cots = lax.all_gather(cotangent, "expert", axis=0, tiled=True)
    hits = (expert_ids[:, :, None] == jnp.arange(groups, dtype=jnp.int32)[None, None, :])
    gates = jnp.sum(jnp.where(hits, gate_probs.astype(jnp.float32)[:, :, None], 0.0), axis=1)
    gates = lax.all_to_all(
        gates.astype(jnp.bfloat16).T.reshape(groups, tok_rows), "expert", 0, 0, tiled=True
    )
    gate_col = gates.reshape(-1).astype(jnp.float32)[:, None]
    full_in = lax.all_gather(w_in[0], "dp", axis=0, tiled=True)
    full_out = lax.all_gather(w_out[0], "dp", axis=0, tiled=True)

    pre = dot(rows, full_in, ((1,), (0,)))
    gate_part = pre[:, :FF]
    up_part = pre[:, FF:]
    sig_part = jax.nn.sigmoid(gate_part)
    activated = gate_part * sig_part
    hidden = (activated * up_part).astype(jnp.bfloat16)
    out_grad = (gate_col * cots.astype(jnp.float32)).astype(jnp.bfloat16)
    term_out = dot(hidden, out_grad, ((0,), (0,))).astype(jnp.bfloat16)
    grad_out = lax.psum_scatter(term_out, "dp", scatter_dimension=0, tiled=True)
    expert_out = dot(hidden, full_out, ((1,), (0,)))
    weighted = (gate_col * expert_out).astype(jnp.bfloat16)
    slot_gate = jnp.sum(cots.astype(jnp.float32) * expert_out, axis=-1).astype(jnp.bfloat16)
    layer_out = lax.psum_scatter(weighted, "expert", scatter_dimension=0, tiled=True)
    gate_back = lax.all_to_all(slot_gate.reshape(groups, tok_rows), "expert", 0, 0, tiled=True)
    hidden_grad = dot(out_grad, full_out, ((1,), (1,)))
    slope = sig_part * (1.0 + gate_part * (1.0 - sig_part))
    pre_grad = jnp.concatenate(
        [hidden_grad * up_part * slope, hidden_grad * activated], axis=-1
    ).astype(jnp.bfloat16)
    term_in = dot(rows, pre_grad, ((0,), (0,))).astype(jnp.bfloat16)
    grad_in = lax.psum_scatter(term_in, "dp", scatter_dimension=0, tiled=True)
    slot_grad = dot(pre_grad, full_in, ((1,), (1,))).astype(jnp.bfloat16)
    tokens_grad = lax.psum_scatter(slot_grad, "expert", scatter_dimension=0, tiled=True)
    gate_grad = jnp.sum(
        jnp.where(hits, gate_back.astype(jnp.float32).T[:, None, :], 0.0), axis=2
    ).astype(jnp.bfloat16)
    w_in_new, mom_in_new = lion_update(w_in, mom_in, grad_in.astype(jnp.float32)[None])
    w_out_new, mom_out_new = lion_update(w_out, mom_out, grad_out.astype(jnp.float32)[None])
    return (layer_out, tokens_grad, gate_grad, w_in_new, w_out_new, mom_in_new, mom_out_new)


def fused_kernel(nz, tok_hbm, cot_hbm, gates_hbm, win_hbm, wout_hbm,
                 layer_ref, tokg_ref, sg_ref, gin_ref, gout_ref,
                 rows, cots, gall, win, wout, ab, hid, hg, wt, pr, up, dn, tin, tout,
                 gi1, gi2, go1, go2, sgs, sgr,
                 loc_sem, ch_send, ch_recv, pt_send, pt_recv, g_send, g_recv,
                 w_send, w_recv, pr_send, pr_recv, rs_send, rs_recv, sg_send, sg_recv,
                 gr_send, gr_recv):
    f32, bf16 = jnp.float32, jnp.bfloat16
    d, e = lax.axis_index("dp"), lax.axis_index("expert")
    z, c = e // 2, e % 2
    ne = 2 * nz
    T = tok_hbm.shape[0]
    D = tok_hbm.shape[1]
    DI, FO = win_hbm.shape[0], wout_hbm.shape[0]
    nb_x, nb_y, nb_g = d + 1 - 2 * (d % 2), (d + 2) % 4, 3 - d
    partner = e + 1 - 2 * c
    above, below = (d, e + 2), (d, e - 2)

    def blk(index):
        return pl.ds(pl.multiple_of(index * T, T), T)

    def remote(src, dst, send, recv, dev):
        return pltpu.make_async_remote_copy(
            src_ref=src, dst_ref=dst, send_sem=send, recv_sem=recv,
            device_id=dev, device_id_type=pl.DeviceIdType.MESH)

    barrier = pltpu.get_barrier_semaphore()
    for k in range(1, ne):
        pl.semaphore_signal(barrier, inc=1, device_id=(d, (e + k) % ne),
                            device_id_type=pl.DeviceIdType.MESH)
    for nb in (nb_x, nb_y):
        pl.semaphore_signal(barrier, inc=1, device_id=(nb, e),
                            device_id_type=pl.DeviceIdType.MESH)

    locs = [
        pltpu.make_async_copy(tok_hbm, rows.at[blk(e)], loc_sem.at[0]),
        pltpu.make_async_copy(win_hbm, win.at[pl.ds(pl.multiple_of(d * DI, DI), DI)], loc_sem.at[1]),
        pltpu.make_async_copy(gates_hbm, gall.at[blk(e)], loc_sem.at[2]),
        pltpu.make_async_copy(cot_hbm, cots.at[blk(e)], loc_sem.at[3]),
        pltpu.make_async_copy(wout_hbm, wout.at[pl.ds(pl.multiple_of(d * FO, FO), FO)], loc_sem.at[4]),
    ]
    for cp in locs:
        cp.start()
    pl.semaphore_wait(barrier, ne + 1)

    def ag_copy(a, index, way, s):
        ref = (rows, cots)[a].at[blk(index)]
        dev = above if way == 0 else below
        return remote(ref, ref, ch_send.at[a, way, s], ch_recv.at[a, way, s], dev)

    def pt_copy(a, index, s):
        ref = (rows, cots)[a].at[blk(index)]
        return remote(ref, ref, pt_send.at[a, s], pt_recv.at[a, s], (d, partner))

    def ag_first(a):
        @pl.when(z < nz - 1)
        def _():
            ag_copy(a, e, 0, 0).start()

        @pl.when(z > 0)
        def _():
            ag_copy(a, e, 1, 0).start()

        pt_copy(a, e, 0).start()

    def ag_step(a, s):
        @pl.when(z >= s)
        def _():
            ag_copy(a, e - 2 * s, 0, s - 1).wait_recv()
            if s < nz - 1:
                @pl.when(z < nz - 1)
                def _():
                    ag_copy(a, e - 2 * s, 0, s).start()
            pt_copy(a, e - 2 * s, s).start()

        @pl.when(z + s <= nz - 1)
        def _():
            ag_copy(a, e + 2 * s, 1, s - 1).wait_recv()
            if s < nz - 1:
                @pl.when(z > 0)
                def _():
                    ag_copy(a, e + 2 * s, 1, s).start()
            pt_copy(a, e + 2 * s, nz - 1 + s).start()

    def ag_end(a):
        pt_copy(a, partner, 0).wait_recv()
        pt_copy(a, e, 0).wait_send()
        for s in range(1, nz):
            @pl.when(z >= s)
            def _():
                pt_copy(a, partner - 2 * s, s).wait_recv()
                pt_copy(a, e - 2 * s, s).wait_send()

            @pl.when(z + s <= nz - 1)
            def _():
                pt_copy(a, partner + 2 * s, nz - 1 + s).wait_recv()
                pt_copy(a, e + 2 * s, nz - 1 + s).wait_send()
        for s in range(nz - 1):
            @pl.when((z >= s) & (z < nz - 1))
            def _():
                ag_copy(a, e - 2 * s, 0, s).wait_send()

            @pl.when((z + s <= nz - 1) & (z > 0))
            def _():
                ag_copy(a, e + 2 * s, 1, s).wait_send()

    def w_copy(a, way, s, owner, half):
        ref, n = ((win, DI), (wout, FO))[a]
        part = ref.at[pl.ds(pl.multiple_of(owner * n + half * (n // 2), n // 2), n // 2)]
        return remote(part, part, w_send.at[a, way, s], w_recv.at[a, way, s],
                      ((nb_x, e), (nb_y, e))[way])

    def w_first(a):
        w_copy(a, 0, 0, d, 1).start()
        w_copy(a, 1, 0, d, 0).start()
        w_copy(a, 0, 1, d, 0).start()
        w_copy(a, 1, 1, d, 1).start()

    def w_forward(a):
        w_copy(a, 0, 0, nb_x, 1).wait_recv()
        w_copy(a, 1, 2, nb_x, 1).start()
        w_copy(a, 1, 0, nb_y, 0).wait_recv()
        w_copy(a, 0, 2, nb_y, 0).start()

    def w_end(a):
        w_copy(a, 0, 1, nb_x, 0).wait_recv()
        w_copy(a, 1, 1, nb_y, 1).wait_recv()
        w_copy(a, 0, 2, nb_g, 0).wait_recv()
        w_copy(a, 1, 2, nb_g, 1).wait_recv()
        for way, s, owner, half in ((0, 0, d, 1), (1, 0, d, 0), (0, 1, d, 0), (1, 1, d, 1),
                                    (0, 2, nb_y, 0), (1, 2, nb_x, 1)):
            w_copy(a, way, s, owner, half).wait_send()

    def g_copy(k, index, dev):
        ref = gall.at[blk(index)]
        return remote(ref, ref, g_send.at[k - 1], g_recv.at[k - 1], (d, dev))

    locs[0].wait()
    ag_first(0)
    locs[1].wait()
    w_first(0)
    locs[2].wait()
    for k in range(1, ne):
        g_copy(k, e, (e + k) % ne).start()
    locs[3].wait()
    ag_first(1)
    locs[4].wait()
    w_first(1)
    ag_step(0, 1)
    w_forward(0)
    ag_step(1, 1)
    ag_step(0, 2)
    ag_step(0, 3)
    for k in range(1, ne):
        g_copy(k, (e + ne - k) % ne, (e + k) % ne).wait_recv()
        g_copy(k, e, (e + k) % ne).wait_send()
    ag_end(0)
    w_end(0)
    ag_step(1, 2)
    w_forward(1)

    def gate_of(r, n):
        lane = lax.broadcasted_iota(jnp.int32, (n, 128), 1)
        return jnp.sum(jnp.where(lane == e, gall[r, :].astype(f32), 0.0), axis=1, keepdims=True)

    def mm(a, b, ca, cb):
        return lax.dot_general(a, b, (((ca,), (cb,)), ((), ())), preferred_element_type=f32)

    M1, N1 = 512, 256
    col_steps = FF // N1
    R = ne * T

    def pre_step(i, carry):
        r = pl.ds(pl.multiple_of((i // col_steps) * M1, M1), M1)
        n = (i % col_steps) * N1
        cg = pl.ds(pl.multiple_of(n, N1), N1)
        cu = pl.ds(pl.multiple_of(n + FF, N1), N1)
        x = rows[r, :]
        gp = mm(x, win[:, cg], 1, 0)
        upp = mm(x, win[:, cu], 1, 0)
        sig = jax.nn.sigmoid(gp)
        act = gp * sig
        h = act * upp
        hid[r, cg] = h.astype(bf16)
        hg[r, cg] = (h * gate_of(r, M1)).astype(bf16)
        ab[r, cg] = (upp * sig * (1.0 + gp * (1.0 - sig))).astype(bf16)
        ab[r, cu] = act.astype(bf16)
        return carry

    lax.fori_loop(0, R // M1 * col_steps, pre_step, 0)
    ag_step(1, 3)
    ag_end(1)

    def term_out_step(i, carry):
        n = pl.ds(pl.multiple_of(i * 512, 512), 512)
        tout[:, n] = mm(hg[...], cots[:, n], 0, 0).astype(bf16)
        return carry

    lax.fori_loop(0, D // 512, term_out_step, 0)

    terms = ((tin, DI, gi1, gi2, gin_ref), (tout, FO, go1, go2, gout_ref))

    def part(a, owner, half):
        ref, n = terms[a][0], terms[a][1]
        return ref.at[pl.ds(pl.multiple_of(owner * n + half * (n // 2), n // 2), n // 2)]

    def gr_copy(a, way, s):
        _, n, first, second, _ = terms[a]
        h = n // 2
        dev = ((nb_x, e), (nb_y, e))[way]
        owner = (nb_x, nb_y)[way]
        if s == 0:
            src, dst = part(a, nb_g, 1 - way), first.at[way]
        else:
            half = (1 - way) if s == 1 else way
            src, dst = part(a, owner, half), second.at[way, pl.ds(half * h, h)]
        return remote(src, dst, gr_send.at[a, way, s], gr_recv.at[a, way, s], dev)

    def gr_sum(a, way):
        gr_copy(a, 1 - way, 0).wait_recv()
        p = part(a, (nb_x, nb_y)[way], way)
        p[...] = (p[...].astype(f32) + terms[a][2][1 - way].astype(f32)).astype(bf16)
        gr_copy(a, way, 2).start()

    def gr_end(a):
        second, out = terms[a][3], terms[a][4]
        h = terms[a][1] // 2
        for half in range(2):
            total = part(a, d, half)[...].astype(f32)
            for way in range(2):
                gr_copy(a, way, 1 if half == 1 - way else 2).wait_recv()
                total = total + second[way, half * h:(half + 1) * h, :].astype(f32)
            out[half * h:(half + 1) * h, :] = total.astype(bf16)
        for way in range(2):
            for s in range(3):
                gr_copy(a, way, s).wait_send()

    for way in range(2):
        gr_copy(1, way, 0).start()
    for way in range(2):
        gr_copy(1, way, 1).start()

    w_end(1)

    def weighted_step(i, carry):
        r = pl.ds(pl.multiple_of((i // 2) * 256, 256), 256)
        n = pl.ds(pl.multiple_of((i % 2) * 1024, 1024), 1024)
        wt[r, n] = mm(hg[r, :], wout[:, n], 1, 0).astype(bf16)
        return carry

    lax.fori_loop(0, R // 256 * 2, weighted_step, 0)

    results = ((wt, layer_ref), (cots, tokg_ref))

    def pr_copy(a, zz):
        return remote(results[a][0].at[blk(2 * zz + 1 - c)], pr.at[a, zz],
                      pr_send.at[a, zz], pr_recv.at[a, zz], (d, partner))

    def pr_first(a):
        for zz in range(nz):
            pr_copy(a, zz).start()

    def pr_end(a):
        for zz in range(nz):
            pr_copy(a, zz).wait()

    def mine(a, b):
        return results[a][0][blk(2 * b + c), :].astype(f32) + pr[a, b].astype(f32)

    def rs_copy(a, way, k, src=None):
        ref = (up, dn)[way]
        src = ref.at[a, k % (nz - 1)] if src is None else src
        return remote(src, ref.at[a, k - 1], rs_send.at[a, way, k - 1],
                      rs_recv.at[a, way, k - 1], (above, below)[way])

    def rs_step(a, k):
        for way in range(2):
            ref = (up, dn)[way]
            has = (z + k <= nz - 1) if way == 0 else (z - k >= 0)
            inner = (z > 0) if way == 0 else (z < nz - 1)
            b = z + k if way == 0 else z - k
            if k < nz - 1:
                @pl.when(has & inner)
                def _():
                    rs_copy(a, way, k + 1).wait_recv()
                    ref[a, k] = (mine(a, b) + ref[a, k].astype(f32)).astype(bf16)
                    rs_copy(a, way, k).start()

            @pl.when(has & jnp.logical_not(inner))
            def _():
                pr[a, b] = mine(a, b).astype(bf16)
                rs_copy(a, way, k, pr.at[a, b]).start()

    def rs_end(a):
        out = results[a][1]

        @pl.when(z == 0)
        def _():
            rs_copy(a, 1, 1).wait_recv()
            out[...] = (mine(a, z) + dn[a, 0].astype(f32)).astype(bf16)

        @pl.when(z == nz - 1)
        def _():
            rs_copy(a, 0, 1).wait_recv()
            out[...] = (mine(a, z) + up[a, 0].astype(f32)).astype(bf16)

        @pl.when((z > 0) & (z < nz - 1))
        def _():
            rs_copy(a, 1, 1).wait_recv()
            rs_copy(a, 0, 1).wait_recv()
            out[...] = (mine(a, z) + up[a, 0].astype(f32) + dn[a, 0].astype(f32)).astype(bf16)

        for k in range(1, nz):
            @pl.when(z + k <= nz - 1)
            def _():
                rs_copy(a, 0, k).wait_send()

            @pl.when(z - k >= 0)
            def _():
                rs_copy(a, 1, k).wait_send()

    pr_first(0)

    def back_step(i, carry):
        r = pl.ds(pl.multiple_of(i * 256, 256), 256)
        q = mm(cots[r, :], wout[...], 1, 1)
        sg = jnp.sum(hid[r, :].astype(f32) * q, axis=1, keepdims=True)
        lane = lax.broadcasted_iota(jnp.int32, (256, 128), 1)
        sgs[r, :] = jnp.where(lane == e, sg, 0.0)
        gq = gate_of(r, 256) * q
        ab[r, :FF] = (gq * ab[r, :FF].astype(f32)).astype(bf16)
        ab[r, FF:] = (gq * ab[r, FF:].astype(f32)).astype(bf16)
        return carry

    lax.fori_loop(0, R // 256, back_step, 0)

    def sg_copy(k):
        to = (e + k) % ne
        return remote(sgs.at[blk(to)], sgr.at[k - 1], sg_send.at[k - 1], sg_recv.at[k - 1], (d, to))

    for k in range(1, ne):
        sg_copy(k).start()
    for way in range(2):
        gr_sum(1, way)
    pr_end(0)
    rs_step(0, 3)

    def term_in(i):
        owner = jnp.where(i < 2, nb_g, jnp.where(i < 6, jnp.where(i % 2 == 0, nb_x, nb_y), d))
        half = jnp.where((i == 2) | (i == 0) | (i == 5) | (i == 7), 1, 0)
        h = DI // 2
        at = pl.ds(pl.multiple_of(owner * DI + half * h, h), h)
        tin[at, :] = mm(rows[:, at], ab[...], 0, 0).astype(bf16)

    def slot_step(i, carry):
        r = pl.ds(pl.multiple_of((i // 2) * 256, 256), 256)
        n = pl.ds(pl.multiple_of((i % 2) * 1024, 1024), 1024)
        cots[r, n] = mm(ab[r, :], win[n, :], 1, 1).astype(bf16)
        return carry

    def term_loop(lo, hi):
        def step(i, carry):
            term_in(i)
            return carry

        lax.fori_loop(lo, hi, step, 0)

    term_loop(0, 4)
    for s in range(2):
        for way in range(2):
            gr_copy(0, way, s).start()
    rs_step(0, 2)
    term_loop(4, 8)
    lax.fori_loop(0, R // 256 * 2, slot_step, 0)
    pr_first(1)
    for way in range(2):
        gr_sum(0, way)
    rs_step(0, 1)
    pr_end(1)
    rs_step(1, 3)
    rs_step(1, 2)
    rs_end(0)
    for k in range(1, ne):
        sg_copy(k).wait()
    acc = sgs[blk(e), :]
    for k in range(1, ne):
        acc = acc + sgr[k - 1]
    sg_ref[...] = acc
    gr_end(1)
    rs_step(1, 1)
    rs_end(1)
    gr_end(0)


def fused_call(nz, tokens, cotangent, gates, w_in, w_out):
    bf16, f32 = jnp.bfloat16, jnp.float32
    T, D = tokens.shape
    DI, F2 = w_in.shape
    FO = w_out.shape[0]
    ne = 2 * nz
    R = ne * T
    dma = pltpu.SemaphoreType.DMA
    return pl.pallas_call(
        functools.partial(fused_kernel, nz),
        out_shape=(
            jax.ShapeDtypeStruct((T, D), bf16),
            jax.ShapeDtypeStruct((T, D), bf16),
            jax.ShapeDtypeStruct((T, 128), f32),
            jax.ShapeDtypeStruct((DI, F2), bf16),
            jax.ShapeDtypeStruct((FO, D), bf16),
        ),
        in_specs=[pl.BlockSpec(memory_space=pl.ANY)] * 5,
        out_specs=tuple([pl.BlockSpec(memory_space=pltpu.VMEM)] * 5),
        scratch_shapes=[
            pltpu.VMEM((R, D), bf16), pltpu.VMEM((R, D), bf16), pltpu.VMEM((R, 128), bf16),
            pltpu.VMEM((4 * DI, F2), bf16), pltpu.VMEM((4 * FO, D), bf16),
            pltpu.VMEM((R, F2), bf16), pltpu.VMEM((R, FF), bf16), pltpu.VMEM((R, FF), bf16),
            pltpu.VMEM((R, D), bf16),
            pltpu.VMEM((2, nz, T, D), bf16), pltpu.VMEM((2, nz - 1, T, D), bf16),
            pltpu.VMEM((2, nz - 1, T, D), bf16),
            pltpu.VMEM((4 * DI, F2), bf16), pltpu.VMEM((4 * FO, D), bf16),
            pltpu.VMEM((2, DI // 2, F2), bf16), pltpu.VMEM((2, DI, F2), bf16),
            pltpu.VMEM((2, FO // 2, D), bf16), pltpu.VMEM((2, FO, D), bf16),
            pltpu.VMEM((R, 128), f32), pltpu.VMEM((ne - 1, T, 128), f32),
            dma((5,)), dma((2, 2, nz - 1)), dma((2, 2, nz - 1)),
            dma((2, 2 * nz - 1)), dma((2, 2 * nz - 1)), dma((ne - 1,)), dma((ne - 1,)),
            dma((2, 2, 3)), dma((2, 2, 3)), dma((2, nz)), dma((2, nz)),
            dma((2, 2, nz - 1)), dma((2, 2, nz - 1)), dma((ne - 1,)), dma((ne - 1,)),
            dma((2, 2, 3)), dma((2, 2, 3)),
        ],
        compiler_params=pltpu.CompilerParams(
            collective_id=0, has_side_effects=True, vmem_limit_bytes=63 * 1024 * 1024),
        cost_estimate=pl.CostEstimate(
            flops=36 * R * D * FF, bytes_accessed=20 * 1024 * 1024, transcendentals=R * FF),
    )(tokens, cotangent, gates, w_in, w_out)


def fused_body(tokens, cotangent, expert_ids, gate_probs, w_in, w_out, mom_in, mom_out):
    groups = lax.axis_size("expert")
    hits = expert_ids[:, :, None] == jnp.arange(128, dtype=jnp.int32)[None, None, :]
    gates = jnp.sum(
        jnp.where(hits, gate_probs.astype(jnp.float32)[:, :, None], 0.0), axis=1
    ).astype(jnp.bfloat16)
    layer_out, tokens_grad, slot_gate, grad_in, grad_out = fused_call(
        groups // 2, tokens, cotangent, gates, w_in[0], w_out[0]
    )
    gate_grad = jnp.sum(jnp.where(hits, slot_gate[:, None, :], 0.0), axis=2).astype(jnp.bfloat16)
    w_in_new, mom_in_new = lion_update(w_in, mom_in, grad_in.astype(jnp.float32)[None])
    w_out_new, mom_out_new = lion_update(w_out, mom_out, grad_out.astype(jnp.float32)[None])
    return (layer_out, tokens_grad, gate_grad, w_in_new, w_out_new, mom_in_new, mom_out_new)


def solution(mesh):
    rows_spec = P(("dp", "expert"), None)
    weight_spec = P("expert", "dp", None)
    in_specs = (rows_spec,) * 4 + (weight_spec,) * 4
    out_specs = (rows_spec,) * 3 + (weight_spec,) * 4
    fits = mesh.shape["dp"] == 4 and mesh.shape["expert"] == 8
    return jax.shard_map(
        fused_body if fits else body,
        mesh=mesh, in_specs=in_specs, out_specs=out_specs, check_vma=False,
    )
```

```python
import functools

import jax
import jax.numpy as jnp
from jax import lax
from jax.experimental import pallas as pl
from jax.experimental.pallas import tpu as pltpu
from jax.sharding import PartitionSpec as P

FF = 768


beta_one = 0.9
beta_two = 0.99
learn_rate = 0.02
decay_rate = 0.1


def lion_update(weight, moment, grad):
    blend = beta_one * moment + (1.0 - beta_one) * grad
    direction = blend / jnp.sqrt(blend * blend + 1.0)
    wide = weight.astype(jnp.float32)
    new_weight = (wide - learn_rate * (direction + decay_rate * wide)).astype(jnp.bfloat16)
    new_moment = beta_two * moment + (1.0 - beta_two) * grad
    return (new_weight, new_moment)


def dot(a, b, contract):
    return lax.dot_general(a, b, (contract, ((), ())), preferred_element_type=jnp.float32)


def body(tokens, cotangent, expert_ids, gate_probs, w_in, w_out, mom_in, mom_out):
    groups = lax.axis_size("expert")
    me = lax.axis_index("expert")
    tok_rows = tokens.shape[0]
    rows = lax.all_gather(tokens, "expert", axis=0, tiled=True)
    cots = lax.all_gather(cotangent, "expert", axis=0, tiled=True)
    hits = (expert_ids[:, :, None] == jnp.arange(groups, dtype=jnp.int32)[None, None, :])
    gates = jnp.sum(jnp.where(hits, gate_probs.astype(jnp.float32)[:, :, None], 0.0), axis=1)
    gates = lax.all_to_all(
        gates.astype(jnp.bfloat16).T.reshape(groups, tok_rows), "expert", 0, 0, tiled=True
    )
    gate_col = gates.reshape(-1).astype(jnp.float32)[:, None]
    full_in = lax.all_gather(w_in[0], "dp", axis=0, tiled=True)
    full_out = lax.all_gather(w_out[0], "dp", axis=0, tiled=True)

    pre = dot(rows, full_in, ((1,), (0,)))
    gate_part = pre[:, :FF]
    up_part = pre[:, FF:]
    sig_part = jax.nn.sigmoid(gate_part)
    activated = gate_part * sig_part
    hidden = (activated * up_part).astype(jnp.bfloat16)
    out_grad = (gate_col * cots.astype(jnp.float32)).astype(jnp.bfloat16)
    term_out = dot(hidden, out_grad, ((0,), (0,))).astype(jnp.bfloat16)
    grad_out = lax.psum_scatter(term_out, "dp", scatter_dimension=0, tiled=True)
    expert_out = dot(hidden, full_out, ((1,), (0,)))
    weighted = (gate_col * expert_out).astype(jnp.bfloat16)
    slot_gate = jnp.sum(cots.astype(jnp.float32) * expert_out, axis=-1).astype(jnp.bfloat16)
    layer_out = lax.psum_scatter(weighted, "expert", scatter_dimension=0, tiled=True)
    gate_back = lax.all_to_all(slot_gate.reshape(groups, tok_rows), "expert", 0, 0, tiled=True)
    hidden_grad = dot(out_grad, full_out, ((1,), (1,)))
    slope = sig_part * (1.0 + gate_part * (1.0 - sig_part))
    pre_grad = jnp.concatenate(
        [hidden_grad * up_part * slope, hidden_grad * activated], axis=-1
    ).astype(jnp.bfloat16)
    term_in = dot(rows, pre_grad, ((0,), (0,))).astype(jnp.bfloat16)
    grad_in = lax.psum_scatter(term_in, "dp", scatter_dimension=0, tiled=True)
    slot_grad = dot(pre_grad, full_in, ((1,), (1,))).astype(jnp.bfloat16)
    tokens_grad = lax.psum_scatter(slot_grad, "expert", scatter_dimension=0, tiled=True)
    gate_grad = jnp.sum(
        jnp.where(hits, gate_back.astype(jnp.float32).T[:, None, :], 0.0), axis=2
    ).astype(jnp.bfloat16)
    w_in_new, mom_in_new = lion_update(w_in, mom_in, grad_in.astype(jnp.float32)[None])
    w_out_new, mom_out_new = lion_update(w_out, mom_out, grad_out.astype(jnp.float32)[None])
    return (layer_out, tokens_grad, gate_grad, w_in_new, w_out_new, mom_in_new, mom_out_new)


def fused_kernel(nz, tok_hbm, cot_hbm, gates_hbm, win_hbm, wout_hbm,
                 layer_ref, tokg_ref, sg_ref, gin_ref, gout_ref,
                 rows, cots, gall, win, wout, ab, hid, hg, wt, pr, up, dn, tin, tout,
                 gi1, gi2, go1, go2, sgs, sgr,
                 loc_sem, ch_send, ch_recv, pt_send, pt_recv, g_send, g_recv,
                 w_send, w_recv, pr_send, pr_recv, rs_send, rs_recv, sg_send, sg_recv,
                 gr_send, gr_recv):
    f32, bf16 = jnp.float32, jnp.bfloat16
    d, e = lax.axis_index("dp"), lax.axis_index("expert")
    z, c = e // 2, e % 2
    ne = 2 * nz
    T = tok_hbm.shape[0]
    D = tok_hbm.shape[1]
    DI, FO = win_hbm.shape[0], wout_hbm.shape[0]
    nb_x, nb_y, nb_g = d + 1 - 2 * (d % 2), (d + 2) % 4, 3 - d
    partner = e + 1 - 2 * c
    above, below = (d, e + 2), (d, e - 2)

    def blk(index):
        return pl.ds(pl.multiple_of(index * T, T), T)

    def remote(src, dst, send, recv, dev):
        return pltpu.make_async_remote_copy(
            src_ref=src, dst_ref=dst, send_sem=send, recv_sem=recv,
            device_id=dev, device_id_type=pl.DeviceIdType.MESH)

    barrier = pltpu.get_barrier_semaphore()
    for k in range(1, ne):
        pl.semaphore_signal(barrier, inc=1, device_id=(d, (e + k) % ne),
                            device_id_type=pl.DeviceIdType.MESH)
    for nb in (nb_x, nb_y):
        pl.semaphore_signal(barrier, inc=1, device_id=(nb, e),
                            device_id_type=pl.DeviceIdType.MESH)

    locs = [
        pltpu.make_async_copy(tok_hbm, rows.at[blk(e)], loc_sem.at[0]),
        pltpu.make_async_copy(win_hbm, win.at[pl.ds(pl.multiple_of(d * DI, DI), DI)], loc_sem.at[1]),
        pltpu.make_async_copy(gates_hbm, gall.at[blk(e)], loc_sem.at[2]),
        pltpu.make_async_copy(cot_hbm, cots.at[blk(e)], loc_sem.at[3]),
        pltpu.make_async_copy(wout_hbm, wout.at[pl.ds(pl.multiple_of(d * FO, FO), FO)], loc_sem.at[4]),
    ]
    for cp in locs:
        cp.start()
    pl.semaphore_wait(barrier, ne + 1)

    def ag_copy(a, index, way, s):
        ref = (rows, cots)[a].at[blk(index)]
        dev = above if way == 0 else below
        return remote(ref, ref, ch_send.at[a, way, s], ch_recv.at[a, way, s], dev)

    def pt_copy(a, index, s):
        ref = (rows, cots)[a].at[blk(index)]
        return remote(ref, ref, pt_send.at[a, s], pt_recv.at[a, s], (d, partner))

    def ag_first(a):
        @pl.when(z < nz - 1)
        def _():
            ag_copy(a, e, 0, 0).start()

        @pl.when(z > 0)
        def _():
            ag_copy(a, e, 1, 0).start()

        pt_copy(a, e, 0).start()

    def ag_step(a, s):
        @pl.when(z >= s)
        def _():
            ag_copy(a, e - 2 * s, 0, s - 1).wait_recv()
            if s < nz - 1:
                @pl.when(z < nz - 1)
                def _():
                    ag_copy(a, e - 2 * s, 0, s).start()
            pt_copy(a, e - 2 * s, s).start()

        @pl.when(z + s <= nz - 1)
        def _():
            ag_copy(a, e + 2 * s, 1, s - 1).wait_recv()
            if s < nz - 1:
                @pl.when(z > 0)
                def _():
                    ag_copy(a, e + 2 * s, 1, s).start()
            pt_copy(a, e + 2 * s, nz - 1 + s).start()

    def ag_end(a):
        pt_copy(a, partner, 0).wait_recv()
        for s in range(1, nz):
            @pl.when(z >= s)
            def _():
                pt_copy(a, partner - 2 * s, s).wait_recv()

            @pl.when(z + s <= nz - 1)
            def _():
                pt_copy(a, partner + 2 * s, nz - 1 + s).wait_recv()

    def ag_sent(a):
        pt_copy(a, e, 0).wait_send()
        for s in range(1, nz):
            @pl.when(z >= s)
            def _():
                pt_copy(a, e - 2 * s, s).wait_send()

            @pl.when(z + s <= nz - 1)
            def _():
                pt_copy(a, e + 2 * s, nz - 1 + s).wait_send()
        for s in range(nz - 1):
            @pl.when((z >= s) & (z < nz - 1))
            def _():
                ag_copy(a, e - 2 * s, 0, s).wait_send()

            @pl.when((z + s <= nz - 1) & (z > 0))
            def _():
                ag_copy(a, e + 2 * s, 1, s).wait_send()

    def w_copy(a, way, s, owner, half):
        ref, n = ((win, DI), (wout, FO))[a]
        part = ref.at[pl.ds(pl.multiple_of(owner * n + half * (n // 2), n // 2), n // 2)]
        return remote(part, part, w_send.at[a, way, s], w_recv.at[a, way, s],
                      ((nb_x, e), (nb_y, e))[way])

    def w_first(a):
        w_copy(a, 0, 0, d, 1).start()
        w_copy(a, 1, 0, d, 0).start()
        w_copy(a, 0, 1, d, 0).start()
        w_copy(a, 1, 1, d, 1).start()

    def w_forward(a):
        w_copy(a, 0, 0, nb_x, 1).wait_recv()
        w_copy(a, 1, 2, nb_x, 1).start()
        w_copy(a, 1, 0, nb_y, 0).wait_recv()
        w_copy(a, 0, 2, nb_y, 0).start()

    def w_middle(a):
        w_copy(a, 0, 1, nb_x, 0).wait_recv()
        w_copy(a, 1, 1, nb_y, 1).wait_recv()

    def w_end(a):
        w_copy(a, 0, 2, nb_g, 0).wait_recv()
        w_copy(a, 1, 2, nb_g, 1).wait_recv()

    def w_sent(a):
        for way, s, owner, half in ((0, 0, d, 1), (1, 0, d, 0), (0, 1, d, 0), (1, 1, d, 1),
                                    (0, 2, nb_y, 0), (1, 2, nb_x, 1)):
            w_copy(a, way, s, owner, half).wait_send()

    def g_copy(k, index, dev):
        ref = gall.at[blk(index)]
        return remote(ref, ref, g_send.at[k - 1], g_recv.at[k - 1], (d, dev))

    locs[0].wait()
    ag_first(0)
    locs[1].wait()
    w_first(0)
    locs[2].wait()
    for k in range(1, ne):
        g_copy(k, e, (e + k) % ne).start()
    locs[3].wait()
    locs[4].wait()
    ag_step(0, 1)
    w_forward(0)
    ag_step(0, 2)
    ag_first(1)
    w_middle(0)
    w_first(1)
    ag_step(0, 3)
    for k in range(1, ne):
        g_copy(k, (e + ne - k) % ne, (e + k) % ne).wait_recv()
        g_copy(k, e, (e + k) % ne).wait_send()
    ag_end(0)
    ag_step(1, 1)
    w_end(0)

    def gate_of(r, n):
        lane = lax.broadcasted_iota(jnp.int32, (n, 128), 1)
        return jnp.sum(jnp.where(lane == e, gall[r, :].astype(f32), 0.0), axis=1, keepdims=True)

    def mm(a, b, ca, cb):
        return lax.dot_general(a, b, (((ca,), (cb,)), ((), ())), preferred_element_type=f32)

    M1, N1 = 512, 256
    col_steps = FF // N1
    R = ne * T

    def pre_step(i, carry):
        r = pl.ds(pl.multiple_of((i // col_steps) * M1, M1), M1)
        n = (i % col_steps) * N1
        cg = pl.ds(pl.multiple_of(n, N1), N1)
        cu = pl.ds(pl.multiple_of(n + FF, N1), N1)
        x = rows[r, :]
        gp = mm(x, win[:, cg], 1, 0)
        upp = mm(x, win[:, cu], 1, 0)
        sig = jax.nn.sigmoid(gp)
        act = gp * sig
        h = act * upp
        hid[r, cg] = h.astype(bf16)
        hg[r, cg] = (h * gate_of(r, M1)).astype(bf16)
        ab[r, cg] = (upp * sig * (1.0 + gp * (1.0 - sig))).astype(bf16)
        ab[r, cu] = act.astype(bf16)
        return carry

    pre_steps = R // M1 * col_steps
    lax.fori_loop(0, pre_steps // 3, pre_step, 0)
    w_forward(1)
    lax.fori_loop(pre_steps // 3, pre_steps * 2 // 3, pre_step, 0)
    ag_step(1, 2)
    lax.fori_loop(pre_steps * 2 // 3, pre_steps, pre_step, 0)
    ag_step(1, 3)
    ag_end(1)

    def term_out_step(i, carry):
        n = pl.ds(pl.multiple_of(i * 512, 512), 512)
        tout[:, n] = mm(hg[...], cots[:, n], 0, 0).astype(bf16)
        return carry

    lax.fori_loop(0, D // 512, term_out_step, 0)

    terms = ((tin, DI, gi1, gi2, gin_ref), (tout, FO, go1, go2, gout_ref))

    def part(a, owner, half):
        ref, n = terms[a][0], terms[a][1]
        return ref.at[pl.ds(pl.multiple_of(owner * n + half * (n // 2), n // 2), n // 2)]

    def gr_copy(a, way, s):
        _, n, first, second, _ = terms[a]
        h = n // 2
        dev = ((nb_x, e), (nb_y, e))[way]
        owner = (nb_x, nb_y)[way]
        if s == 0:
            src, dst = part(a, nb_g, 1 - way), first.at[way]
        else:
            half = (1 - way) if s == 1 else way
            src, dst = part(a, owner, half), second.at[way, pl.ds(half * h, h)]
        return remote(src, dst, gr_send.at[a, way, s], gr_recv.at[a, way, s], dev)

    def gr_sum(a, way):
        gr_copy(a, 1 - way, 0).wait_recv()
        p = part(a, (nb_x, nb_y)[way], way)
        p[...] = (p[...].astype(f32) + terms[a][2][1 - way].astype(f32)).astype(bf16)
        gr_copy(a, way, 2).start()

    def gr_end(a):
        second, out = terms[a][3], terms[a][4]
        h = terms[a][1] // 2
        for half in range(2):
            total = part(a, d, half)[...].astype(f32)
            for way in range(2):
                gr_copy(a, way, 1 if half == 1 - way else 2).wait_recv()
                total = total + second[way, half * h:(half + 1) * h, :].astype(f32)
            out[half * h:(half + 1) * h, :] = total.astype(bf16)
        for way in range(2):
            for s in range(3):
                gr_copy(a, way, s).wait_send()

    for way in range(2):
        gr_copy(1, way, 0).start()
    for way in range(2):
        gr_copy(1, way, 1).start()

    w_middle(1)
    w_end(1)

    def weighted_step(i, carry):
        r = pl.ds(pl.multiple_of((i // 2) * 256, 256), 256)
        n = pl.ds(pl.multiple_of((i % 2) * 1024, 1024), 1024)
        wt[r, n] = mm(hg[r, :], wout[:, n], 1, 0).astype(bf16)
        return carry

    lax.fori_loop(0, R // 256 * 2, weighted_step, 0)

    results = ((wt, layer_ref), (cots, tokg_ref))

    def pr_copy(a, zz):
        return remote(results[a][0].at[blk(2 * zz + 1 - c)], pr.at[a, zz],
                      pr_send.at[a, zz], pr_recv.at[a, zz], (d, partner))

    def pr_first(a):
        for zz in range(nz):
            pr_copy(a, zz).start()

    def pr_end(a):
        for zz in range(nz):
            pr_copy(a, zz).wait()

    def mine(a, b):
        return results[a][0][blk(2 * b + c), :].astype(f32) + pr[a, b].astype(f32)

    def rs_copy(a, way, k, src=None):
        ref = (up, dn)[way]
        src = ref.at[a, k % (nz - 1)] if src is None else src
        return remote(src, ref.at[a, k - 1], rs_send.at[a, way, k - 1],
                      rs_recv.at[a, way, k - 1], (above, below)[way])

    def rs_step(a, k):
        for way in range(2):
            ref = (up, dn)[way]
            has = (z + k <= nz - 1) if way == 0 else (z - k >= 0)
            inner = (z > 0) if way == 0 else (z < nz - 1)
            b = z + k if way == 0 else z - k
            if k < nz - 1:
                @pl.when(has & inner)
                def _():
                    rs_copy(a, way, k + 1).wait_recv()
                    ref[a, k] = (mine(a, b) + ref[a, k].astype(f32)).astype(bf16)
                    rs_copy(a, way, k).start()

            @pl.when(has & jnp.logical_not(inner))
            def _():
                pr[a, b] = mine(a, b).astype(bf16)
                rs_copy(a, way, k, pr.at[a, b]).start()

    def rs_end(a):
        out = results[a][1]

        @pl.when(z == 0)
        def _():
            rs_copy(a, 1, 1).wait_recv()
            out[...] = (mine(a, z) + dn[a, 0].astype(f32)).astype(bf16)

        @pl.when(z == nz - 1)
        def _():
            rs_copy(a, 0, 1).wait_recv()
            out[...] = (mine(a, z) + up[a, 0].astype(f32)).astype(bf16)

        @pl.when((z > 0) & (z < nz - 1))
        def _():
            rs_copy(a, 1, 1).wait_recv()
            rs_copy(a, 0, 1).wait_recv()
            out[...] = (mine(a, z) + up[a, 0].astype(f32) + dn[a, 0].astype(f32)).astype(bf16)

        for k in range(1, nz):
            @pl.when(z + k <= nz - 1)
            def _():
                rs_copy(a, 0, k).wait_send()

            @pl.when(z - k >= 0)
            def _():
                rs_copy(a, 1, k).wait_send()

    pr_first(0)

    def back_step(i, carry):
        r = pl.ds(pl.multiple_of(i * 256, 256), 256)
        q = mm(cots[r, :], wout[...], 1, 1)
        sg = jnp.sum(hid[r, :].astype(f32) * q, axis=1, keepdims=True)
        lane = lax.broadcasted_iota(jnp.int32, (256, 128), 1)
        sgs[r, :] = jnp.where(lane == e, sg, 0.0)
        gq = gate_of(r, 256) * q
        ab[r, :FF] = (gq * ab[r, :FF].astype(f32)).astype(bf16)
        ab[r, FF:] = (gq * ab[r, FF:].astype(f32)).astype(bf16)
        return carry

    lax.fori_loop(0, R // 256, back_step, 0)

    def sg_copy(k):
        to = (e + k) % ne
        return remote(sgs.at[blk(to)], sgr.at[k - 1], sg_send.at[k - 1], sg_recv.at[k - 1], (d, to))

    for k in range(1, ne):
        sg_copy(k).start()
    for way in range(2):
        gr_sum(1, way)
    pr_end(0)
    rs_step(0, 3)

    def term_in(i):
        owner = jnp.where(i < 2, nb_g, jnp.where(i < 6, jnp.where(i % 2 == 0, nb_x, nb_y), d))
        half = jnp.where((i == 2) | (i == 0) | (i == 5) | (i == 7), 1, 0)
        h = DI // 2
        at = pl.ds(pl.multiple_of(owner * DI + half * h, h), h)
        tin[at, :] = mm(rows[:, at], ab[...], 0, 0).astype(bf16)

    def slot_step(i, carry):
        r = pl.ds(pl.multiple_of((i // 2) * 256, 256), 256)
        n = pl.ds(pl.multiple_of((i % 2) * 1024, 1024), 1024)
        cots[r, n] = mm(ab[r, :], win[n, :], 1, 1).astype(bf16)
        return carry

    def term_loop(lo, hi):
        def step(i, carry):
            term_in(i)
            return carry

        lax.fori_loop(lo, hi, step, 0)

    term_loop(0, 4)
    for s in range(2):
        for way in range(2):
            gr_copy(0, way, s).start()
    term_loop(4, 8)
    rs_step(0, 2)
    ag_sent(1)
    lax.fori_loop(0, R // 256 * 2, slot_step, 0)
    pr_first(1)
    rs_step(0, 1)
    pr_end(1)
    rs_step(1, 3)
    for way in range(2):
        gr_sum(0, way)
    rs_end(0)
    for k in range(1, ne):
        sg_copy(k).wait()
    acc = sgs[blk(e), :]
    for k in range(1, ne):
        acc = acc + sgr[k - 1]
    sg_ref[...] = acc
    rs_step(1, 2)
    gr_end(1)
    rs_step(1, 1)
    rs_end(1)
    ag_sent(0)
    w_sent(0)
    w_sent(1)
    gr_end(0)


def fused_call(nz, tokens, cotangent, gates, w_in, w_out):
    bf16, f32 = jnp.bfloat16, jnp.float32
    T, D = tokens.shape
    DI, F2 = w_in.shape
    FO = w_out.shape[0]
    ne = 2 * nz
    R = ne * T
    dma = pltpu.SemaphoreType.DMA
    return pl.pallas_call(
        functools.partial(fused_kernel, nz),
        out_shape=(
            jax.ShapeDtypeStruct((T, D), bf16),
            jax.ShapeDtypeStruct((T, D), bf16),
            jax.ShapeDtypeStruct((T, 128), f32),
            jax.ShapeDtypeStruct((DI, F2), bf16),
            jax.ShapeDtypeStruct((FO, D), bf16),
        ),
        in_specs=[pl.BlockSpec(memory_space=pl.ANY)] * 5,
        out_specs=tuple([pl.BlockSpec(memory_space=pltpu.VMEM)] * 5),
        scratch_shapes=[
            pltpu.VMEM((R, D), bf16), pltpu.VMEM((R, D), bf16), pltpu.VMEM((R, 128), bf16),
            pltpu.VMEM((4 * DI, F2), bf16), pltpu.VMEM((4 * FO, D), bf16),
            pltpu.VMEM((R, F2), bf16), pltpu.VMEM((R, FF), bf16), pltpu.VMEM((R, FF), bf16),
            pltpu.VMEM((R, D), bf16),
            pltpu.VMEM((2, nz, T, D), bf16), pltpu.VMEM((2, nz - 1, T, D), bf16),
            pltpu.VMEM((2, nz - 1, T, D), bf16),
            pltpu.VMEM((4 * DI, F2), bf16), pltpu.VMEM((4 * FO, D), bf16),
            pltpu.VMEM((2, DI // 2, F2), bf16), pltpu.VMEM((2, DI, F2), bf16),
            pltpu.VMEM((2, FO // 2, D), bf16), pltpu.VMEM((2, FO, D), bf16),
            pltpu.VMEM((R, 128), f32), pltpu.VMEM((ne - 1, T, 128), f32),
            dma((5,)), dma((2, 2, nz - 1)), dma((2, 2, nz - 1)),
            dma((2, 2 * nz - 1)), dma((2, 2 * nz - 1)), dma((ne - 1,)), dma((ne - 1,)),
            dma((2, 2, 3)), dma((2, 2, 3)), dma((2, nz)), dma((2, nz)),
            dma((2, 2, nz - 1)), dma((2, 2, nz - 1)), dma((ne - 1,)), dma((ne - 1,)),
            dma((2, 2, 3)), dma((2, 2, 3)),
        ],
        compiler_params=pltpu.CompilerParams(
            collective_id=0, has_side_effects=True, vmem_limit_bytes=63 * 1024 * 1024),
        cost_estimate=pl.CostEstimate(
            flops=36 * R * D * FF, bytes_accessed=20 * 1024 * 1024, transcendentals=R * FF),
    )(tokens, cotangent, gates, w_in, w_out)


def fused_body(tokens, cotangent, expert_ids, gate_probs, w_in, w_out, mom_in, mom_out):
    groups = lax.axis_size("expert")
    hits = expert_ids[:, :, None] == jnp.arange(128, dtype=jnp.int32)[None, None, :]
    gates = jnp.sum(
        jnp.where(hits, gate_probs.astype(jnp.float32)[:, :, None], 0.0), axis=1
    ).astype(jnp.bfloat16)
    layer_out, tokens_grad, slot_gate, grad_in, grad_out = fused_call(
        groups // 2, tokens, cotangent, gates, w_in[0], w_out[0]
    )
    gate_grad = jnp.sum(jnp.where(hits, slot_gate[:, None, :], 0.0), axis=2).astype(jnp.bfloat16)
    w_in_new, mom_in_new = lion_update(w_in, mom_in, grad_in.astype(jnp.float32)[None])
    w_out_new, mom_out_new = lion_update(w_out, mom_out, grad_out.astype(jnp.float32)[None])
    return (layer_out, tokens_grad, gate_grad, w_in_new, w_out_new, mom_in_new, mom_out_new)


def solution(mesh):
    rows_spec = P(("dp", "expert"), None)
    weight_spec = P("expert", "dp", None)
    in_specs = (rows_spec,) * 4 + (weight_spec,) * 4
    out_specs = (rows_spec,) * 3 + (weight_spec,) * 4
    fits = mesh.shape["dp"] == 4 and mesh.shape["expert"] == 8
    return jax.shard_map(
        fused_body if fits else body,
        mesh=mesh, in_specs=in_specs, out_specs=out_specs, check_vma=False,
    )
```

```python
import functools

import jax
import jax.numpy as jnp
from jax import lax
from jax.experimental import pallas as pl
from jax.experimental.pallas import tpu as pltpu
from jax.sharding import PartitionSpec as P

FF = 768


beta_one = 0.9
beta_two = 0.99
learn_rate = 0.02
decay_rate = 0.1


def lion_update(weight, moment, grad):
    blend = beta_one * moment + (1.0 - beta_one) * grad
    direction = blend * lax.rsqrt(blend * blend + 1.0)
    wide = weight.astype(jnp.float32)
    new_weight = (wide - learn_rate * (direction + decay_rate * wide)).astype(jnp.bfloat16)
    new_moment = beta_two * moment + (1.0 - beta_two) * grad
    return (new_weight, new_moment)


def dot(a, b, contract):
    return lax.dot_general(a, b, (contract, ((), ())), preferred_element_type=jnp.float32)


def body(tokens, cotangent, expert_ids, gate_probs, w_in, w_out, mom_in, mom_out):
    groups = lax.axis_size("expert")
    me = lax.axis_index("expert")
    tok_rows = tokens.shape[0]
    rows = lax.all_gather(tokens, "expert", axis=0, tiled=True)
    cots = lax.all_gather(cotangent, "expert", axis=0, tiled=True)
    hits = (expert_ids[:, :, None] == jnp.arange(groups, dtype=jnp.int32)[None, None, :])
    gates = jnp.sum(jnp.where(hits, gate_probs.astype(jnp.float32)[:, :, None], 0.0), axis=1)
    gates = lax.all_to_all(
        gates.astype(jnp.bfloat16).T.reshape(groups, tok_rows), "expert", 0, 0, tiled=True
    )
    gate_col = gates.reshape(-1).astype(jnp.float32)[:, None]
    full_in = lax.all_gather(w_in[0], "dp", axis=0, tiled=True)
    full_out = lax.all_gather(w_out[0], "dp", axis=0, tiled=True)

    pre = dot(rows, full_in, ((1,), (0,)))
    gate_part = pre[:, :FF]
    up_part = pre[:, FF:]
    sig_part = jax.nn.sigmoid(gate_part)
    activated = gate_part * sig_part
    hidden = (activated * up_part).astype(jnp.bfloat16)
    out_grad = (gate_col * cots.astype(jnp.float32)).astype(jnp.bfloat16)
    term_out = dot(hidden, out_grad, ((0,), (0,))).astype(jnp.bfloat16)
    grad_out = lax.psum_scatter(term_out, "dp", scatter_dimension=0, tiled=True)
    expert_out = dot(hidden, full_out, ((1,), (0,)))
    weighted = (gate_col * expert_out).astype(jnp.bfloat16)
    slot_gate = jnp.sum(cots.astype(jnp.float32) * expert_out, axis=-1).astype(jnp.bfloat16)
    layer_out = lax.psum_scatter(weighted, "expert", scatter_dimension=0, tiled=True)
    gate_back = lax.all_to_all(slot_gate.reshape(groups, tok_rows), "expert", 0, 0, tiled=True)
    hidden_grad = dot(out_grad, full_out, ((1,), (1,)))
    slope = sig_part * (1.0 + gate_part * (1.0 - sig_part))
    pre_grad = jnp.concatenate(
        [hidden_grad * up_part * slope, hidden_grad * activated], axis=-1
    ).astype(jnp.bfloat16)
    term_in = dot(rows, pre_grad, ((0,), (0,))).astype(jnp.bfloat16)
    grad_in = lax.psum_scatter(term_in, "dp", scatter_dimension=0, tiled=True)
    slot_grad = dot(pre_grad, full_in, ((1,), (1,))).astype(jnp.bfloat16)
    tokens_grad = lax.psum_scatter(slot_grad, "expert", scatter_dimension=0, tiled=True)
    gate_grad = jnp.sum(
        jnp.where(hits, gate_back.astype(jnp.float32).T[:, None, :], 0.0), axis=2
    ).astype(jnp.bfloat16)
    w_in_new, mom_in_new = lion_update(w_in, mom_in, grad_in.astype(jnp.float32)[None])
    w_out_new, mom_out_new = lion_update(w_out, mom_out, grad_out.astype(jnp.float32)[None])
    return (layer_out, tokens_grad, gate_grad, w_in_new, w_out_new, mom_in_new, mom_out_new)


def fused_kernel(nz, tok_hbm, cot_hbm, win_hbm, wout_hbm, ids_ref, probs_ref,
                 layer_ref, tokg_ref, sg_ref, gin_ref, gout_ref,
                 rows, cots, gall, win, wout, ab, hid, hg, wt, pr, up, dn, tin, tout,
                 gi1, gi2, go1, go2, sgs, sgr,
                 loc_sem, ch_send, ch_recv, pt_send, pt_recv, g_send, g_recv,
                 w_send, w_recv, pr_send, pr_recv, rs_send, rs_recv, sg_send, sg_recv,
                 gr_send, gr_recv):
    f32, bf16 = jnp.float32, jnp.bfloat16
    d, e = lax.axis_index("dp"), lax.axis_index("expert")
    z, c = e // 2, e % 2
    ne = 2 * nz
    T = tok_hbm.shape[0]
    D = tok_hbm.shape[1]
    DI, FO = win_hbm.shape[0], wout_hbm.shape[0]
    nb_x, nb_y, nb_g = d + 1 - 2 * (d % 2), (d + 2) % 4, 3 - d
    partner = e + 1 - 2 * c
    above, below = (d, e + 2), (d, e - 2)

    def blk(index):
        return pl.ds(pl.multiple_of(index * T, T), T)

    def remote(src, dst, send, recv, dev):
        return pltpu.make_async_remote_copy(
            src_ref=src, dst_ref=dst, send_sem=send, recv_sem=recv,
            device_id=dev, device_id_type=pl.DeviceIdType.MESH)

    barrier = pltpu.get_barrier_semaphore()
    for k in range(1, ne):
        pl.semaphore_signal(barrier, inc=1, device_id=(d, (e + k) % ne),
                            device_id_type=pl.DeviceIdType.MESH)
    for nb in (nb_x, nb_y):
        pl.semaphore_signal(barrier, inc=1, device_id=(nb, e),
                            device_id_type=pl.DeviceIdType.MESH)

    locs = [
        pltpu.make_async_copy(tok_hbm, rows.at[blk(e)], loc_sem.at[0]),
        pltpu.make_async_copy(win_hbm, win.at[pl.ds(pl.multiple_of(d * DI, DI), DI)], loc_sem.at[1]),
        pltpu.make_async_copy(cot_hbm, cots.at[blk(e)], loc_sem.at[2]),
        pltpu.make_async_copy(wout_hbm, wout.at[pl.ds(pl.multiple_of(d * FO, FO), FO)], loc_sem.at[3]),
    ]
    for cp in locs:
        cp.start()
    lanes = lax.broadcasted_iota(jnp.int32, (T, 128), 1)
    picks = [lanes == ids_ref[:, k:k + 1] for k in range(ids_ref.shape[1])]
    dense = jnp.zeros((T, 128), f32)
    for k, pick in enumerate(picks):
        dense = jnp.where(pick, probs_ref[:, k:k + 1].astype(f32), dense)
    gall[blk(e), :] = dense.astype(bf16)
    pl.semaphore_wait(barrier, ne + 1)

    def ag_copy(a, index, way, s):
        ref = (rows, cots)[a].at[blk(index)]
        dev = above if way == 0 else below
        return remote(ref, ref, ch_send.at[a, way, s], ch_recv.at[a, way, s], dev)

    def pt_copy(a, index, s):
        ref = (rows, cots)[a].at[blk(index)]
        return remote(ref, ref, pt_send.at[a, s], pt_recv.at[a, s], (d, partner))

    def ag_first(a):
        @pl.when(z < nz - 1)
        def _():
            ag_copy(a, e, 0, 0).start()

        @pl.when(z > 0)
        def _():
            ag_copy(a, e, 1, 0).start()

        pt_copy(a, e, 0).start()

    def ag_step(a, s):
        @pl.when(z >= s)
        def _():
            ag_copy(a, e - 2 * s, 0, s - 1).wait_recv()
            if s < nz - 1:
                @pl.when(z < nz - 1)
                def _():
                    ag_copy(a, e - 2 * s, 0, s).start()
            pt_copy(a, e - 2 * s, s).start()

        @pl.when(z + s <= nz - 1)
        def _():
            ag_copy(a, e + 2 * s, 1, s - 1).wait_recv()
            if s < nz - 1:
                @pl.when(z > 0)
                def _():
                    ag_copy(a, e + 2 * s, 1, s).start()
            pt_copy(a, e + 2 * s, nz - 1 + s).start()

    def ag_end(a):
        pt_copy(a, partner, 0).wait_recv()
        for s in range(1, nz):
            @pl.when(z >= s)
            def _():
                pt_copy(a, partner - 2 * s, s).wait_recv()

            @pl.when(z + s <= nz - 1)
            def _():
                pt_copy(a, partner + 2 * s, nz - 1 + s).wait_recv()

    def ag_sent(a):
        pt_copy(a, e, 0).wait_send()
        for s in range(1, nz):
            @pl.when(z >= s)
            def _():
                pt_copy(a, e - 2 * s, s).wait_send()

            @pl.when(z + s <= nz - 1)
            def _():
                pt_copy(a, e + 2 * s, nz - 1 + s).wait_send()
        for s in range(nz - 1):
            @pl.when((z >= s) & (z < nz - 1))
            def _():
                ag_copy(a, e - 2 * s, 0, s).wait_send()

            @pl.when((z + s <= nz - 1) & (z > 0))
            def _():
                ag_copy(a, e + 2 * s, 1, s).wait_send()

    def w_copy(a, way, s, owner, half):
        ref, n = ((win, DI), (wout, FO))[a]
        part = ref.at[pl.ds(pl.multiple_of(owner * n + half * (n // 2), n // 2), n // 2)]
        return remote(part, part, w_send.at[a, way, s], w_recv.at[a, way, s],
                      ((nb_x, e), (nb_y, e))[way])

    def w_first(a):
        w_copy(a, 0, 0, d, 1).start()
        w_copy(a, 1, 0, d, 0).start()
        w_copy(a, 0, 1, d, 0).start()
        w_copy(a, 1, 1, d, 1).start()

    def w_forward(a):
        w_copy(a, 0, 0, nb_x, 1).wait_recv()
        w_copy(a, 1, 2, nb_x, 1).start()
        w_copy(a, 1, 0, nb_y, 0).wait_recv()
        w_copy(a, 0, 2, nb_y, 0).start()

    def w_middle(a):
        w_copy(a, 0, 1, nb_x, 0).wait_recv()
        w_copy(a, 1, 1, nb_y, 1).wait_recv()

    def w_end(a):
        w_copy(a, 0, 2, nb_g, 0).wait_recv()
        w_copy(a, 1, 2, nb_g, 1).wait_recv()

    def w_sent(a):
        for way, s, owner, half in ((0, 0, d, 1), (1, 0, d, 0), (0, 1, d, 0), (1, 1, d, 1),
                                    (0, 2, nb_y, 0), (1, 2, nb_x, 1)):
            w_copy(a, way, s, owner, half).wait_send()

    def g_copy(k, index, dev):
        ref = gall.at[blk(index)]
        return remote(ref, ref, g_send.at[k - 1], g_recv.at[k - 1], (d, dev))

    locs[0].wait()
    ag_first(0)
    locs[1].wait()
    w_first(0)
    for k in range(1, ne):
        g_copy(k, e, (e + k) % ne).start()
    locs[2].wait()
    locs[3].wait()
    ag_step(0, 1)
    w_forward(0)
    ag_step(0, 2)
    ag_first(1)
    w_middle(0)
    w_first(1)
    ag_step(0, 3)
    for k in range(1, ne):
        g_copy(k, (e + ne - k) % ne, (e + k) % ne).wait_recv()
        g_copy(k, e, (e + k) % ne).wait_send()
    ag_end(0)
    ag_step(1, 1)
    w_end(0)

    def gate_of(r, n):
        lane = lax.broadcasted_iota(jnp.int32, (n, 128), 1)
        return jnp.sum(jnp.where(lane == e, gall[r, :].astype(f32), 0.0), axis=1, keepdims=True)

    def mm(a, b, ca, cb):
        return lax.dot_general(a, b, (((ca,), (cb,)), ((), ())), preferred_element_type=f32)

    M1, N1 = 512, 256
    col_steps = FF // N1
    R = ne * T

    def pre_step(i, carry):
        r = pl.ds(pl.multiple_of((i // col_steps) * M1, M1), M1)
        n = (i % col_steps) * N1
        cg = pl.ds(pl.multiple_of(n, N1), N1)
        cu = pl.ds(pl.multiple_of(n + FF, N1), N1)
        x = rows[r, :]
        gp = mm(x, win[:, cg], 1, 0)
        upp = mm(x, win[:, cu], 1, 0)
        sig = jax.nn.sigmoid(gp)
        act = gp * sig
        h = act * upp
        hid[r, cg] = h.astype(bf16)
        hg[r, cg] = (h * gate_of(r, M1)).astype(bf16)
        ab[r, cg] = (upp * sig * (1.0 + gp * (1.0 - sig))).astype(bf16)
        ab[r, cu] = act.astype(bf16)
        return carry

    pre_steps = R // M1 * col_steps
    lax.fori_loop(0, pre_steps // 3, pre_step, 0)
    w_forward(1)
    lax.fori_loop(pre_steps // 3, pre_steps * 2 // 3, pre_step, 0)
    ag_step(1, 2)
    lax.fori_loop(pre_steps * 2 // 3, pre_steps, pre_step, 0)
    ag_step(1, 3)
    ag_end(1)

    def term_out_step(i, carry):
        n = pl.ds(pl.multiple_of(i * 512, 512), 512)
        tout[:, n] = mm(hg[...], cots[:, n], 0, 0).astype(bf16)
        return carry

    lax.fori_loop(0, D // 512, term_out_step, 0)

    terms = ((tin, DI, gi1, gi2, gin_ref), (tout, FO, go1, go2, gout_ref))

    def part(a, owner, half):
        ref, n = terms[a][0], terms[a][1]
        return ref.at[pl.ds(pl.multiple_of(owner * n + half * (n // 2), n // 2), n // 2)]

    def gr_copy(a, way, s):
        _, n, first, second, _ = terms[a]
        h = n // 2
        dev = ((nb_x, e), (nb_y, e))[way]
        owner = (nb_x, nb_y)[way]
        if s == 0:
            src, dst = part(a, nb_g, 1 - way), first.at[way]
        else:
            half = (1 - way) if s == 1 else way
            src, dst = part(a, owner, half), second.at[way, pl.ds(half * h, h)]
        return remote(src, dst, gr_send.at[a, way, s], gr_recv.at[a, way, s], dev)

    def gr_sum(a, way):
        gr_copy(a, 1 - way, 0).wait_recv()
        p = part(a, (nb_x, nb_y)[way], way)
        p[...] = (p[...].astype(f32) + terms[a][2][1 - way].astype(f32)).astype(bf16)
        gr_copy(a, way, 2).start()

    def gr_end(a):
        second, out = terms[a][3], terms[a][4]
        h = terms[a][1] // 2
        for half in range(2):
            total = part(a, d, half)[...].astype(f32)
            for way in range(2):
                gr_copy(a, way, 1 if half == 1 - way else 2).wait_recv()
                total = total + second[way, half * h:(half + 1) * h, :].astype(f32)
            out[half * h:(half + 1) * h, :] = total.astype(bf16)
        for way in range(2):
            for s in range(3):
                gr_copy(a, way, s).wait_send()

    for way in range(2):
        gr_copy(1, way, 0).start()
    for way in range(2):
        gr_copy(1, way, 1).start()

    w_middle(1)
    w_end(1)

    def weighted_step(i, carry):
        r = pl.ds(pl.multiple_of((i // 2) * 256, 256), 256)
        n = pl.ds(pl.multiple_of((i % 2) * 1024, 1024), 1024)
        wt[r, n] = mm(hg[r, :], wout[:, n], 1, 0).astype(bf16)
        return carry

    lax.fori_loop(0, R // 256 * 2, weighted_step, 0)

    results = ((wt, layer_ref), (cots, tokg_ref))

    def pr_copy(a, zz):
        return remote(results[a][0].at[blk(2 * zz + 1 - c)], pr.at[a, zz],
                      pr_send.at[a, zz], pr_recv.at[a, zz], (d, partner))

    def pr_first(a):
        for zz in range(nz):
            pr_copy(a, zz).start()

    def pr_end(a):
        for zz in range(nz):
            pr_copy(a, zz).wait()

    def mine(a, b):
        return results[a][0][blk(2 * b + c), :].astype(f32) + pr[a, b].astype(f32)

    def rs_copy(a, way, k, src=None):
        ref = (up, dn)[way]
        src = ref.at[a, k % (nz - 1)] if src is None else src
        return remote(src, ref.at[a, k - 1], rs_send.at[a, way, k - 1],
                      rs_recv.at[a, way, k - 1], (above, below)[way])

    def rs_step(a, k):
        for way in range(2):
            ref = (up, dn)[way]
            has = (z + k <= nz - 1) if way == 0 else (z - k >= 0)
            inner = (z > 0) if way == 0 else (z < nz - 1)
            b = z + k if way == 0 else z - k
            if k < nz - 1:
                @pl.when(has & inner)
                def _():
                    rs_copy(a, way, k + 1).wait_recv()
                    ref[a, k] = (mine(a, b) + ref[a, k].astype(f32)).astype(bf16)
                    rs_copy(a, way, k).start()

            @pl.when(has & jnp.logical_not(inner))
            def _():
                pr[a, b] = mine(a, b).astype(bf16)
                rs_copy(a, way, k, pr.at[a, b]).start()

    def rs_end(a):
        out = results[a][1]

        @pl.when(z == 0)
        def _():
            rs_copy(a, 1, 1).wait_recv()
            out[...] = (mine(a, z) + dn[a, 0].astype(f32)).astype(bf16)

        @pl.when(z == nz - 1)
        def _():
            rs_copy(a, 0, 1).wait_recv()
            out[...] = (mine(a, z) + up[a, 0].astype(f32)).astype(bf16)

        @pl.when((z > 0) & (z < nz - 1))
        def _():
            rs_copy(a, 1, 1).wait_recv()
            rs_copy(a, 0, 1).wait_recv()
            out[...] = (mine(a, z) + up[a, 0].astype(f32) + dn[a, 0].astype(f32)).astype(bf16)

        for k in range(1, nz):
            @pl.when(z + k <= nz - 1)
            def _():
                rs_copy(a, 0, k).wait_send()

            @pl.when(z - k >= 0)
            def _():
                rs_copy(a, 1, k).wait_send()

    pr_first(0)

    def back_step(i, carry):
        r = pl.ds(pl.multiple_of(i * 256, 256), 256)
        q = mm(cots[r, :], wout[...], 1, 1)
        sg = jnp.sum(hid[r, :].astype(f32) * q, axis=1, keepdims=True)
        lane = lax.broadcasted_iota(jnp.int32, (256, 128), 1)
        sgs[r, :] = jnp.where(lane == e, sg, 0.0)
        gq = gate_of(r, 256) * q
        ab[r, :FF] = (gq * ab[r, :FF].astype(f32)).astype(bf16)
        ab[r, FF:] = (gq * ab[r, FF:].astype(f32)).astype(bf16)
        return carry

    lax.fori_loop(0, R // 256, back_step, 0)

    def sg_copy(k):
        to = (e + k) % ne
        return remote(sgs.at[blk(to)], sgr.at[k - 1], sg_send.at[k - 1], sg_recv.at[k - 1], (d, to))

    for k in range(1, ne):
        sg_copy(k).start()
    for way in range(2):
        gr_sum(1, way)
    pr_end(0)
    rs_step(0, 3)

    def term_in(i):
        owner = jnp.where(i < 2, nb_g, jnp.where(i < 6, jnp.where(i % 2 == 0, nb_x, nb_y), d))
        half = jnp.where((i == 2) | (i == 0) | (i == 5) | (i == 7), 1, 0)
        h = DI // 2
        at = pl.ds(pl.multiple_of(owner * DI + half * h, h), h)
        tin[at, :] = mm(rows[:, at], ab[...], 0, 0).astype(bf16)

    def slot_step(i, carry):
        r = pl.ds(pl.multiple_of((i // 2) * 256, 256), 256)
        n = pl.ds(pl.multiple_of((i % 2) * 1024, 1024), 1024)
        cots[r, n] = mm(ab[r, :], win[n, :], 1, 1).astype(bf16)
        return carry

    def term_loop(lo, hi):
        def step(i, carry):
            term_in(i)
            return carry

        lax.fori_loop(lo, hi, step, 0)

    term_loop(0, 2)
    for way in range(2):
        gr_copy(0, way, 0).start()
    term_loop(2, 4)
    for way in range(2):
        gr_copy(0, way, 1).start()
    term_loop(4, 6)
    ag_sent(1)
    slot_steps = R // 256 * 2
    lax.fori_loop(0, slot_steps // 2, slot_step, 0)
    rs_step(0, 2)
    lax.fori_loop(slot_steps // 2, slot_steps, slot_step, 0)
    pr_first(1)
    rs_step(0, 1)
    term_loop(6, 8)
    pr_end(1)
    rs_step(1, 3)
    for way in range(2):
        gr_sum(0, way)
    rs_end(0)
    for k in range(1, ne):
        sg_copy(k).wait()
    acc = sgs[blk(e), :]
    for k in range(1, ne):
        acc = acc + sgr[k - 1]
    top_lane = lax.broadcasted_iota(jnp.int32, (T, len(picks)), 1)
    back = jnp.zeros((T, len(picks)), f32)
    for k in range(len(picks)):
        pick = lanes == ids_ref[:, k:k + 1]
        value = jnp.sum(jnp.where(pick, acc, 0.0), axis=1, keepdims=True)
        back = jnp.where(top_lane == k, value, back)
    sg_ref[...] = back.astype(bf16)
    rs_step(1, 2)
    gr_end(1)
    rs_step(1, 1)
    rs_end(1)
    ag_sent(0)
    w_sent(0)
    w_sent(1)
    gr_end(0)


def fused_call(nz, tokens, cotangent, w_in, w_out, expert_ids, gate_probs):
    bf16, f32 = jnp.bfloat16, jnp.float32
    T, D = tokens.shape
    DI, F2 = w_in.shape
    FO = w_out.shape[0]
    ne = 2 * nz
    R = ne * T
    dma = pltpu.SemaphoreType.DMA
    return pl.pallas_call(
        functools.partial(fused_kernel, nz),
        out_shape=(
            jax.ShapeDtypeStruct((T, D), bf16),
            jax.ShapeDtypeStruct((T, D), bf16),
            jax.ShapeDtypeStruct(expert_ids.shape, bf16),
            jax.ShapeDtypeStruct((DI, F2), bf16),
            jax.ShapeDtypeStruct((FO, D), bf16),
        ),
        in_specs=[pl.BlockSpec(memory_space=pl.ANY)] * 4
        + [pl.BlockSpec(memory_space=pltpu.VMEM)] * 2,
        out_specs=tuple([pl.BlockSpec(memory_space=pltpu.VMEM)] * 5),
        scratch_shapes=[
            pltpu.VMEM((R, D), bf16), pltpu.VMEM((R, D), bf16), pltpu.VMEM((R, 128), bf16),
            pltpu.VMEM((4 * DI, F2), bf16), pltpu.VMEM((4 * FO, D), bf16),
            pltpu.VMEM((R, F2), bf16), pltpu.VMEM((R, FF), bf16), pltpu.VMEM((R, FF), bf16),
            pltpu.VMEM((R, D), bf16),
            pltpu.VMEM((2, nz, T, D), bf16), pltpu.VMEM((2, nz - 1, T, D), bf16),
            pltpu.VMEM((2, nz - 1, T, D), bf16),
            pltpu.VMEM((4 * DI, F2), bf16), pltpu.VMEM((4 * FO, D), bf16),
            pltpu.VMEM((2, DI // 2, F2), bf16), pltpu.VMEM((2, DI, F2), bf16),
            pltpu.VMEM((2, FO // 2, D), bf16), pltpu.VMEM((2, FO, D), bf16),
            pltpu.VMEM((R, 128), f32), pltpu.VMEM((ne - 1, T, 128), f32),
            dma((4,)), dma((2, 2, nz - 1)), dma((2, 2, nz - 1)),
            dma((2, 2 * nz - 1)), dma((2, 2 * nz - 1)), dma((ne - 1,)), dma((ne - 1,)),
            dma((2, 2, 3)), dma((2, 2, 3)), dma((2, nz)), dma((2, nz)),
            dma((2, 2, nz - 1)), dma((2, 2, nz - 1)), dma((ne - 1,)), dma((ne - 1,)),
            dma((2, 2, 3)), dma((2, 2, 3)),
        ],
        compiler_params=pltpu.CompilerParams(
            collective_id=0, has_side_effects=True, vmem_limit_bytes=63 * 1024 * 1024),
        cost_estimate=pl.CostEstimate(
            flops=36 * R * D * FF, bytes_accessed=20 * 1024 * 1024, transcendentals=R * FF),
    )(tokens, cotangent, w_in, w_out, expert_ids, gate_probs)


def fused_body(tokens, cotangent, expert_ids, gate_probs, w_in, w_out, mom_in, mom_out):
    groups = lax.axis_size("expert")
    layer_out, tokens_grad, gate_grad, grad_in, grad_out = fused_call(
        groups // 2, tokens, cotangent, w_in[0], w_out[0], expert_ids, gate_probs
    )
    w_in_new, mom_in_new = lion_update(w_in, mom_in, grad_in.astype(jnp.float32)[None])
    w_out_new, mom_out_new = lion_update(w_out, mom_out, grad_out.astype(jnp.float32)[None])
    return (layer_out, tokens_grad, gate_grad, w_in_new, w_out_new, mom_in_new, mom_out_new)


def solution(mesh):
    rows_spec = P(("dp", "expert"), None)
    weight_spec = P("expert", "dp", None)
    in_specs = (rows_spec,) * 4 + (weight_spec,) * 4
    out_specs = (rows_spec,) * 3 + (weight_spec,) * 4
    fits = mesh.shape["dp"] == 4 and mesh.shape["expert"] == 8
    return jax.shard_map(
        fused_body if fits else body,
        mesh=mesh, in_specs=in_specs, out_specs=out_specs, check_vma=False,
    )
```
